256 devices in a mesh: chan: 32 (over y, z), day: 8 (over x, core).
Axes of the slice: x: 4, y: 4, z: 8, core: 2. Of those that a mesh axis runs over, the one named last changes fastest.
Arguments:
- segment_records: bfloat16 [16, 512, 24, 2048], P('day', 'chan')
- block_requests: int32 [32, 32, 2], replicated, may hold values from 0 to 15, as said below
- pair_slots: int32 [2048, 2], P('chan'), may hold values from 0 to 63, as said below
Outputs:
- correlations: float32 [2048, 256], P(('chan', 'day'))
The draws below stay inside these ranges and needn't reach their ends.
Inputs may be any that keep to these rules, and one draw needn't show every extreme that they name: `block_requests`: for each owner and each device of chan, 2 different channels of that device, as indices among its 16 channels. `pair_slots`: rows 64 * o to 64 * (o + 1) - 1 are the pairs of owner o; an entry is a slot s * 2 + k of that owner, the k-th channel it requests from device s of chan; the two slots of a pair differ.
All inputs are finite; a program needn't handle non-finite values.
Results may differ from the reference program's by a relative error of at most 0.0051.
Values may be sent and summed in bfloat16 or wider, within the bound.
A program may use at most 256 MiB of HBM per device.

```python
import math
import jax
import jax.numpy as jnp
from jax import lax

L = 2048
F = 1024
LAGS = 256
CAP = 2
CH_DEV = 16
SEGS = 24
PAIR_DEV = 64
OWNERS = 32
SLOTS = 64
CHANNELS = 512
DAYS = 16
PAIRS = 2048


def draw_segment_records(key, part):
    key = jax.random.fold_in(key, 11)
    noise_key, scale_key = jax.random.split(key)
    shape = (DAYS, CHANNELS, SEGS, L)
    noise = jax.random.normal(noise_key, shape, jnp.float32)
    scales = jnp.exp(jax.random.uniform(scale_key, (DAYS, CHANNELS, SEGS, 1), jnp.float32, 0.0, math.log(10.0)))
    return (noise * scales).astype(jnp.bfloat16)


def draw_block_requests(key, part):
    key = jax.random.fold_in(key, 12)
    scores = jax.random.randint(key, (OWNERS, OWNERS, CH_DEV), 0, 2 ** 20) * CH_DEV
    scores = scores + jnp.arange(CH_DEV, dtype=jnp.int32)
    order = jnp.argsort(scores, axis=-1, stable=True)
    return order[..., :CAP].astype(jnp.int32)


def draw_pair_slots(key, part):
    key = jax.random.fold_in(key, 13)
    perm_key, step_key = jax.random.split(key)
    scores = jax.random.randint(perm_key, (OWNERS, SLOTS), 0, 2 ** 20) * SLOTS
    scores = scores + jnp.arange(SLOTS, dtype=jnp.int32)
    order = jnp.argsort(scores, axis=-1, stable=True).astype(jnp.int32)
    firsts = order[:, jnp.arange(PAIR_DEV, dtype=jnp.int32) % SLOTS]
    steps_away = jax.random.randint(step_key, (OWNERS, PAIR_DEV), 1, SLOTS)
    seconds = (firsts + steps_away) % SLOTS
    return jnp.stack([firsts, seconds], axis=-1).reshape(PAIRS, 2).astype(jnp.int32)


def setup_inputs(seed: int = 0) -> dict:
    key_list = jax.random.split(jax.random.key(seed), 4)
    segment_records = draw_segment_records(jax.random.fold_in(key_list[3], 71), 0)
    block_requests = draw_block_requests(jax.random.fold_in(key_list[3], 71), 0)
    pair_slots = draw_pair_slots(jax.random.fold_in(key_list[3], 71), 0)
    return {"segment_records": segment_records, "block_requests": block_requests, "pair_slots": pair_slots}


def forward_table():
    sample_idx = jnp.arange(L, dtype=jnp.int32)[:, None]
    bin_idx = jnp.arange(1, F + 1, dtype=jnp.int32)[None, :]
    phase = (sample_idx * bin_idx % L).astype(jnp.float32) * (2.0 * math.pi / L)
    taper = 0.5 - 0.5 * jnp.cos(jnp.arange(L, dtype=jnp.int32).astype(jnp.float32) * (2.0 * math.pi / L))
    table = jnp.concatenate([taper[:, None] * jnp.cos(phase), -taper[:, None] * jnp.sin(phase)], axis=1)
    return table.astype(jnp.bfloat16)

def lag_table():
    bin_idx = jnp.arange(1, F + 1, dtype=jnp.int32)[:, None]
    lag_idx = jnp.arange(LAGS, dtype=jnp.int32)[None, :] - LAGS // 2
    phase = (bin_idx * lag_idx % L).astype(jnp.float32) * (2.0 * math.pi / L)
    return jnp.concatenate([jnp.cos(phase), -jnp.sin(phase)], axis=0)

def whiten(spectra):
    power = lax.optimization_barrier(jnp.mean(spectra * spectra, axis=-1, keepdims=True))
    real_part = spectra[..., :F]
    imag_part = spectra[..., F:]
    amplitude = jnp.sqrt(real_part * real_part + imag_part * imag_part + 0.02 * power + 1e-06)
    return jnp.concatenate([real_part / amplitude, imag_part / amplitude], axis=-1).astype(jnp.bfloat16)

def cross_parts(left_spec, right_spec):
    left_full = left_spec.astype(jnp.float32)
    right_full = right_spec.astype(jnp.float32)
    left_real, left_imag = (left_full[..., :F], left_full[..., F:])
    right_real, right_imag = (right_full[..., :F], right_full[..., F:])
    real_part = lax.optimization_barrier(jnp.sum(left_real * right_real + left_imag * right_imag, axis=2))
    imag_part = lax.optimization_barrier(jnp.sum(left_imag * right_real - left_real * right_imag, axis=2))
    return jnp.concatenate([real_part, imag_part], axis=-1)

def reference(segment_records, block_requests, pair_slots):
    table = forward_table()

    def one_day(day_records):
        spectra = jnp.dot(day_records.reshape(-1, L), table, preferred_element_type=jnp.float32)
        return whiten(spectra).reshape(CHANNELS, SEGS, 2 * F)
    white = lax.map(one_day, segment_records)
    slot_source = (jnp.arange(SLOTS, dtype=jnp.int32) // CAP)[None, :]
    slot_chan = slot_source * CH_DEV + block_requests.reshape(OWNERS, SLOTS)
    owner_of = jnp.arange(PAIRS, dtype=jnp.int32) // PAIR_DEV
    first_chan = slot_chan[owner_of, pair_slots[:, 0]].reshape(OWNERS, PAIR_DEV)
    second_chan = slot_chan[owner_of, pair_slots[:, 1]].reshape(OWNERS, PAIR_DEV)

    def one_owner(indices):
        left_spec = jnp.take(white, indices[0], axis=1)
        right_spec = jnp.take(white, indices[1], axis=1)
        return lax.optimization_barrier(jnp.sum(cross_parts(left_spec, right_spec), axis=0))
    cross = lax.map(one_owner, (first_chan, second_chan)).reshape(PAIRS, 2 * F)
    norm_scale = 1.0 / math.sqrt(2.0 * DAYS * SEGS * F)
    lagged = jnp.dot(cross, lag_table(), precision=lax.Precision.HIGHEST, preferred_element_type=jnp.float32)
    return lagged * norm_scale
```

```python
import math

import jax
import jax.numpy as jnp
import numpy as np
from jax import lax
from jax.experimental import pallas as pl
from jax.experimental.pallas import tpu as pltpu
from jax.sharding import PartitionSpec as P

L = 2048
F = 1024
LAGS = 256
MESH = pl.DeviceIdType.MESH
NC = 32
BINS = F // NC
NU = NC // 4
NJ = 3
SEG = 8
CH = 16
ROWS = CH * SEG
ND = 8


def forward_blocks():
    n = np.arange(L, dtype=np.int64)[:, None]
    k = np.arange(1, F + 1, dtype=np.int64)[None, :]
    phase = (n * k % L).astype(np.float32) * np.float32(2.0 * math.pi / L)
    taper = np.float32(0.5) - np.float32(0.5) * np.cos(
        np.arange(L, dtype=np.float32) * np.float32(2.0 * math.pi / L)
    )
    real = (taper[:, None] * np.cos(phase)).reshape(L, NU, 4, BINS)
    imag = (-taper[:, None] * np.sin(phase)).reshape(L, NU, 4, BINS)
    both = np.stack([real, imag], axis=2).reshape(L, NU, 256)
    return np.ascontiguousarray(both.transpose(1, 0, 2)).astype(jnp.bfloat16)


def lag_rows():
    k = np.arange(1, F + 1, dtype=np.int64)[:, None]
    t = np.arange(LAGS, dtype=np.int64)[None, :] - LAGS // 2
    phase = (k * t % L).astype(np.float32) * np.float32(2.0 * math.pi / L)
    both = np.stack([np.cos(phase).reshape(NC, BINS, LAGS), -np.sin(phase).reshape(NC, BINS, LAGS)], axis=1)
    both = both.reshape(2 * F, LAGS).astype(np.float32)
    high = both.astype(jnp.bfloat16)
    return np.stack([high, (both - high.astype(np.float32)).astype(jnp.bfloat16)])


def swap(rows, even):
    return jnp.where(even, pltpu.roll(rows, 96, 1), pltpu.roll(rows, 32, 1))


def kernel(
    req, slots, x_hbm, tab_hbm, lag_hbm, out,
    xv, xs, tab, spec, send, recv, lag, mine_s, mine_v, index_v, index, plain, turned, acc1, acc2,
    day_send, day_recv, own_send, own_recv, lhs,
    x_sem, tab_sem, lag_sem, send_sem, recv_sem, index_send_sem, index_recv_sem, smem_sem,
    day_send_sem, day_recv_sem, own_send_sem, own_recv_sem,
):
    me = lax.axis_index("chan")
    day = lax.axis_index("day")
    my_u = me // 4
    lane = lax.broadcasted_iota(jnp.int32, (ROWS, 128), 1)
    even = lane % 64 < 32
    low = lane < 64

    x_copy = pltpu.make_async_copy(x_hbm, xv, x_sem)
    x_copy.start()

    def tab_copy(step):
        u = lax.rem(my_u + step, NU)
        return pltpu.make_async_copy(tab_hbm.at[u], tab.at[u], tab_sem.at[u])

    @pl.loop(0, NU)
    def _(step):
        tab_copy(step).start()

    lag_copy = pltpu.make_async_copy(lag_hbm, lag, lag_sem)
    lag_copy.start()

    barrier = pltpu.get_barrier_semaphore()

    @pl.loop(1, NC)
    def _(i):
        pl.semaphore_signal(
            barrier, inc=1, device_id=(lax.rem(me + i, NC), day), device_id_type=MESH
        )

    @pl.loop(1, ND)
    def _(i):
        pl.semaphore_signal(
            barrier, inc=1, device_id=(me, lax.rem(day + i, ND)), device_id_type=MESH
        )

    @pl.loop(0, 64)
    def _(i):
        for k in range(2):
            slot = slots[k, i]
            source = slot >> 1
            mine_s[k, i] = source * CH + req[me, slot & 1, source]

    mine_copy = pltpu.make_async_copy(mine_s, mine_v, smem_sem)
    mine_copy.start()

    x_copy.wait()

    @pl.loop(0, 16)
    def _(i):
        rows = xv[pl.ds(pl.multiple_of(i * 48, 16), 48), :].astype(jnp.float32).reshape(2, NJ, SEG, L)
        for j in range(NJ):
            xs[j, pl.ds(pl.multiple_of(i * 16, 16), 16), :] = (
                rows[:, j].reshape(16, L).astype(jnp.bfloat16)
            )

    def block_copy(j, to):
        return pltpu.make_async_remote_copy(
            src_ref=send.at[j, to],
            dst_ref=recv.at[j, me],
            send_sem=send_sem.at[j],
            recv_sem=recv_sem.at[j, me],
            device_id=(to, day),
            device_id_type=MESH,
        )

    def index_copy(to):
        return pltpu.make_async_remote_copy(
            src_ref=mine_v,
            dst_ref=index_v.at[me],
            send_sem=index_send_sem,
            recv_sem=index_recv_sem,
            device_id=(to, day),
            device_id_type=MESH,
        )

    for j in range(NJ):

        def transform(step, total):
            u = lax.rem(my_u + step, NU)
            if j == 0:
                tab_copy(step).wait()
            y = jnp.dot(xs[j], tab[u], preferred_element_type=jnp.float32)
            spec[u] = y
            return total + (y[:, :128] * y[:, :128] + y[:, 128:] * y[:, 128:])

        total = lax.fori_loop(0, NU, transform, jnp.zeros((2 * ROWS, 128), jnp.float32))
        floor = jnp.sum(total, axis=-1, keepdims=True) * (0.02 / (2 * F)) + 1e-06

        if j == 0:
            pl.semaphore_wait(barrier, NC - 1 + ND - 1)

        @pl.loop(0, NU)
        def _(step):
            u = lax.rem(my_u + step, NU)
            parts = []
            for d in range(2):
                real = spec[u, d * ROWS : (d + 1) * ROWS, :128]
                imag = spec[u, d * ROWS : (d + 1) * ROWS, 128:]
                scale = lax.rsqrt(real * real + imag * imag + floor[d * ROWS : (d + 1) * ROWS])
                real, imag = real * scale, swap(imag * scale, even)
                if d == 1:
                    real, imag = pltpu.roll(real, 64, 1), pltpu.roll(imag, 64, 1)
                parts += [jnp.where(even, real, imag), jnp.where(even, imag, real)]
            a, b, c, e = parts
            send[j, 4 * u + 0] = jnp.where(low, a, c).astype(jnp.bfloat16)
            send[j, 4 * u + 1] = jnp.where(low, b, e).astype(jnp.bfloat16)
            send[j, 4 * u + 2] = jnp.where(low, c, a).astype(jnp.bfloat16)
            send[j, 4 * u + 3] = jnp.where(low, e, b).astype(jnp.bfloat16)

            @pl.loop(0, 4)
            def _(q):
                to = 4 * u + q

                @pl.when(to != me)
                def _():
                    block_copy(j, to).start()

        if j == 0:
            mine_copy.wait()
            index_v[me] = mine_v[...]

            @pl.loop(1, NC)
            def _(i):
                index_copy(lax.rem(me + i, NC)).start()

    others = pl.ds(0, NC - 1)
    pltpu.make_async_copy(index_v.at[others], index_v.at[others], index_recv_sem).wait()
    index_to_smem = pltpu.make_async_copy(index_v, index, smem_sem)
    index_to_smem.start()
    index_to_smem.wait()

    def arrive(j, to):
        @pl.loop(0, NC)
        def _(i):
            source = lax.rem(lax.rem(my_u - i // 4 + NU, NU) * 4 + lax.rem(i, 4), NC)
            at = pl.ds(pl.multiple_of(source * CH, CH), CH)

            def store(rows):
                rows = rows.astype(jnp.float32)
                plain[to, at] = rows.reshape(CH, SEG, 128)
                turned[to, at] = swap(rows, even).reshape(CH, SEG, 128)

            @pl.when(source != me)
            def _():
                pltpu.make_async_copy(
                    send.at[j, source], recv.at[j, source], recv_sem.at[j, source]
                ).wait()
                store(recv[j, source])

            @pl.when(source == me)
            def _():
                store(send[j, me])

    sign = jnp.where(even, -1.0, 1.0) * (1 - 2 * lax.rem(me, 2)).astype(jnp.float32)

    def group(dd, chunks):
        @pl.loop(0, NC)
        def _(o):
            for r in range(8):
                first, second = index[o, 0, dd * 8 + r], index[o, 1, dd * 8 + r]
                one = two = None
                for j in range(chunks):
                    a = plain[j, first]
                    b, c = a * plain[j, second], a * turned[j, second]
                    one, two = (b, c) if j == 0 else (one + b, two + c)
                at = pl.ds(pl.multiple_of((o * 8 + r) * 8, 8), 8)
                acc1[at, :] = one
                acc2[at, :] = two

        folded = []
        for half in range(2):
            for k, acc in enumerate((acc1, acc2)):
                total = acc[pl.ds(half * 1024, ROWS, stride=8), :]
                for s in range(1, 8):
                    total = total + acc[pl.ds(half * 1024 + s, ROWS, stride=8), :]
                if k == 1:
                    total = total * sign
                total = total + pltpu.roll(total, 64, 1)
                folded.append(total + pltpu.roll(total, 32, 1))
        re_lo, im_lo, re_hi, im_hi = folded
        return jnp.where(low, jnp.where(even, re_lo, im_lo), jnp.where(even, re_hi, im_hi))

    arrive(0, 0)
    arrive(1, 1)

    @pl.loop(0, ND)
    def _(dd):
        day_send[dd] = group(dd, 2)

    arrive(2, 0)

    def day_copy(to):
        return pltpu.make_async_remote_copy(
            src_ref=day_send.at[to],
            dst_ref=day_recv.at[day],
            send_sem=day_send_sem,
            recv_sem=day_recv_sem.at[day],
            device_id=(me, to),
            device_id_type=MESH,
        )

    @pl.loop(1, ND + 1)
    def _(i):
        dd = lax.rem(day + i, ND)
        day_send[dd] = day_send[dd] + group(dd, 1)

        @pl.when(dd != day)
        def _():
            day_copy(dd).start()

    total = day_send[day]
    own_send[...] = total.reshape(16, 8, 128)

    @pl.loop(1, ND)
    def _(i):
        source = lax.rem(day - i + ND, ND)
        pltpu.make_async_copy(day_send.at[source], day_recv.at[source], day_recv_sem.at[source]).wait()
        own_send[...] = own_send[...] + day_recv[source].reshape(16, 8, 128)

    def own_copy(to):
        return pltpu.make_async_remote_copy(
            src_ref=own_send.at[lax.rem(to, 16)],
            dst_ref=own_recv.at[me],
            send_sem=own_send_sem,
            recv_sem=own_recv_sem,
            device_id=(to, day),
            device_id_type=MESH,
        )

    @pl.loop(1, NC)
    def _(i):
        own_copy(lax.rem(me + i, NC)).start()

    own_recv[me] = own_send[lax.rem(me, 16)]

    pltpu.make_async_copy(own_recv.at[others], own_recv.at[others], own_recv_sem).wait()

    upper = (jnp.zeros((8, 128), jnp.int32) + me) >= 16
    narrow = low[:8]
    for t in range(16):
        pair = []
        for s in (2 * t, 2 * t + 1):
            v = own_recv[s]
            turned_v = pltpu.roll(v, 64, 1)
            pair.append(jnp.where(upper, turned_v, v) if s % 2 == 0 else jnp.where(upper, v, turned_v))
        value = jnp.where(narrow, pair[0], pair[1])
        high = value.astype(jnp.bfloat16).astype(jnp.float32)
        lhs[:, t * 128 : (t + 1) * 128] = jnp.concatenate([high, value - high], axis=0).astype(jnp.bfloat16)

    lag_copy.wait()
    lagged = jnp.dot(lhs[...], lag[0], preferred_element_type=jnp.float32) + jnp.dot(
        lhs[...], lag[1], preferred_element_type=jnp.float32
    )
    out[...] = (lagged[:8] + lagged[8:]) * (1.0 / math.sqrt(2.0 * 16 * 24 * F))

    for j in range(NJ):
        pltpu.make_async_copy(send.at[j, others], recv.at[j, others], send_sem.at[j]).wait()
    pltpu.make_async_copy(index_v.at[others], index_v.at[others], index_send_sem).wait()
    pltpu.make_async_copy(own_recv.at[others], own_recv.at[others], own_send_sem).wait()
    days = pl.ds(0, ND - 1)
    pltpu.make_async_copy(day_send.at[days], day_recv.at[days], day_send_sem).wait()


def body(segment_records, block_requests, pair_slots):
    bf16, f32, i32 = jnp.bfloat16, jnp.float32, jnp.int32
    dma = pltpu.SemaphoreType.DMA
    return pl.pallas_call(
        kernel,
        out_shape=jax.ShapeDtypeStruct((8, LAGS), f32),
        in_specs=[
            pl.BlockSpec(memory_space=pltpu.SMEM),
            pl.BlockSpec(memory_space=pltpu.SMEM),
            pl.BlockSpec(memory_space=pl.ANY),
            pl.BlockSpec(memory_space=pl.ANY),
            pl.BlockSpec(memory_space=pl.ANY),
        ],
        out_specs=pl.BlockSpec(memory_space=pltpu.VMEM),
        scratch_shapes=[
            pltpu.VMEM((768, L), bf16),
            pltpu.VMEM((NJ, 256, L), bf16),
            pltpu.VMEM((NU, L, 256), bf16),
            pltpu.VMEM((NU, 256, 256), f32),
            pltpu.VMEM((NJ, NC, ROWS, 128), bf16),
            pltpu.VMEM((NJ, NC, ROWS, 128), bf16),
            pltpu.VMEM((2, 2 * F, LAGS), bf16),
            pltpu.SMEM((2, 64), i32),
            pltpu.VMEM((2, 64), i32),
            pltpu.VMEM((NC, 2, 64), i32),
            pltpu.SMEM((NC, 2, 64), i32),
            pltpu.VMEM((2, NC * CH, SEG, 128), f32),
            pltpu.VMEM((2, NC * CH, SEG, 128), f32),
            pltpu.VMEM((2048, 128), f32),
            pltpu.VMEM((2048, 128), f32),
            pltpu.VMEM((ND, ROWS, 128), f32),
            pltpu.VMEM((ND, ROWS, 128), f32),
            pltpu.VMEM((16, 8, 128), f32),
            pltpu.VMEM((NC, 8, 128), f32),
            pltpu.VMEM((16, 2 * F), bf16),
            dma, dma((NU,)), dma, dma((NJ,)), dma((NJ, NC)), dma, dma, dma,
            dma, dma((ND,)), dma, dma,
        ],
        compiler_params=pltpu.CompilerParams(
            collective_id=0, has_side_effects=True, vmem_limit_bytes=60 * 2**20
        ),
        name="correlate",
    )(
        block_requests.transpose(0, 2, 1),
        pair_slots.T,
        segment_records.reshape(768, L),
        jnp.asarray(forward_blocks()),
        jnp.asarray(lag_rows()),
    )


def solution(mesh):
    return jax.shard_map(
        body,
        mesh=mesh,
        in_specs=(P("day", "chan", None, None), P(), P("chan", None)),
        out_specs=P(("chan", "day"), None),
        check_vma=False,
    )
```

```python
import math

import jax
import jax.numpy as jnp
import numpy as np
from jax import lax
from jax.experimental import pallas as pl
from jax.experimental.pallas import tpu as pltpu
from jax.sharding import PartitionSpec as P

L = 2048
F = 1024
LAGS = 256
MESH = pl.DeviceIdType.MESH
NC = 32
BINS = F // NC
NU = NC // 4
NJ = 3
SEG = 8
CH = 16
ROWS = CH * SEG
ND = 8


def forward_blocks():
    n = np.arange(L, dtype=np.int64)[:, None]
    k = np.arange(1, F + 1, dtype=np.int64)[None, :]
    phase = (n * k % L).astype(np.float32) * np.float32(2.0 * math.pi / L)
    taper = np.float32(0.5) - np.float32(0.5) * np.cos(
        np.arange(L, dtype=np.float32) * np.float32(2.0 * math.pi / L)
    )
    real = (taper[:, None] * np.cos(phase)).reshape(L, NU, 4, BINS)
    imag = (-taper[:, None] * np.sin(phase)).reshape(L, NU, 4, BINS)
    both = np.stack([real, imag], axis=2).reshape(L, NU, 256)
    return np.ascontiguousarray(both.transpose(1, 0, 2)).astype(jnp.bfloat16)


def taper_rows():
    n = np.arange(L, dtype=np.float32)
    taper = np.float32(0.5) - np.float32(0.5) * np.cos(n * np.float32(2.0 * math.pi / L))
    return np.broadcast_to(taper, (8, L)).copy()


def lag_rows():
    k = np.arange(1, F + 1, dtype=np.int64)[:, None]
    t = np.arange(LAGS, dtype=np.int64)[None, :] - LAGS // 2
    phase = (k * t % L).astype(np.float32) * np.float32(2.0 * math.pi / L)
    shape = (NC // 2, 2, BINS, LAGS)
    both = np.stack([np.cos(phase).reshape(shape), -np.sin(phase).reshape(shape)], axis=1)
    both = both.reshape(2 * F, LAGS).astype(np.float32)
    high = both.astype(jnp.bfloat16)
    return np.stack([high, (both - high.astype(np.float32)).astype(jnp.bfloat16)])


def alternate(count, step):
    return count // 2 + (1 - 2 * lax.rem(step, 2)) * ((step + 1) // 2)


def kernel(
    req_hbm, slots_hbm, x_hbm, taper_hbm, tab_hbm, lag_hbm, out,
    req, slots, xv, xs, taper, squares, sums, tab, spec, send, recv, lag, mine_s, mine_v, index_v, index_s, index, forms, acc,
    day_send, day_recv, last_send, last_recv, own_send, own_recv, lhs,
    in_sem, x_sem, taper_sem, tab_sem, lag_sem, send_sem, recv_sem, index_send_sem, index_recv_sem, smem_sem,
    day_send_sem, day_recv_sem, last_send_sem, last_recv_sem, own_send_sem, own_recv_sem,
):
    me = lax.axis_index("chan")
    day = lax.axis_index("day")
    my_u = me // 4
    lane = lax.broadcasted_iota(jnp.int32, (ROWS, 128), 1)
    even = lane % 64 < 32
    low = lane < 64

    def peer(step):
        y = lax.rem(me // 8 + alternate(4, lax.rem(step, 4)), 4)
        z = lax.rem(lax.rem(me, 8) + alternate(8, step // 4), 8)
        return y * 8 + z

    x_copy = pltpu.make_async_copy(x_hbm, xv, x_sem)
    x_copy.start()
    taper_copy = pltpu.make_async_copy(taper_hbm, taper, taper_sem)
    taper_copy.start()
    slots_copy = pltpu.make_async_copy(slots_hbm, slots, in_sem.at[0])
    slots_copy.start()
    req_copy = pltpu.make_async_copy(req_hbm, req, in_sem.at[1])
    req_copy.start()

    barrier = pltpu.get_barrier_semaphore()

    @pl.loop(0, NC - 1)
    def _(i):
        pl.semaphore_signal(barrier, inc=1, device_id=(peer(i), day), device_id_type=MESH)

    @pl.loop(1, ND)
    def _(i):
        pl.semaphore_signal(
            barrier, inc=1, device_id=(me, lax.rem(day + i, ND)), device_id_type=MESH
        )

    def tab_copy(step):
        u = lax.rem(my_u + step, NU)
        return pltpu.make_async_copy(tab_hbm.at[u], tab.at[u], tab_sem.at[u])

    @pl.loop(0, NU)
    def _(step):
        tab_copy(step).start()

    lag_copy = pltpu.make_async_copy(lag_hbm, lag, lag_sem)
    lag_copy.start()

    slots_copy.wait()
    req_copy.wait()

    @pl.loop(0, 64)
    def _(i):
        for k in range(2):
            slot = slots[k, i]
            source = slot >> 1
            mine_s[k, i] = (source * CH + req[me, slot & 1, source]) * 4

    mine_copy = pltpu.make_async_copy(mine_s, mine_v, smem_sem)
    mine_copy.start()

    taper_copy.wait()
    x_copy.wait()

    def gather_rows(chunks):
        @pl.loop(0, 16)
        def _(i):
            rows = xv[pl.ds(pl.multiple_of(i * 48, 16), 48), :].astype(jnp.float32)
            rows = rows.reshape(2, NJ, SEG, L)
            at = pl.ds(pl.multiple_of(i * 16, 16), 16)
            for j in chunks:
                xs[j, at, :] = rows[:, j].reshape(16, L).astype(jnp.bfloat16)
                for half in range(2):
                    tapered = rows[half, j] * taper[...]
                    square = plain = None
                    for t in range(L // 128):
                        part = tapered[:, t * 128 : (t + 1) * 128]
                        square = part * part if t == 0 else square + part * part
                        plain = part if t == 0 else plain + part
                    low_at = pl.ds(pl.multiple_of(i * 16 + half * 8, 8), 8)
                    squares[j, low_at, :] = square
                    sums[j, low_at, :] = plain

    gather_rows((0,))

    def block_copy(j, to):
        return pltpu.make_async_remote_copy(
            src_ref=send.at[j, to],
            dst_ref=recv.at[j, me],
            send_sem=send_sem.at[j],
            recv_sem=recv_sem.at[j, me],
            device_id=(to, day),
            device_id_type=MESH,
        )

    def index_copy(to):
        return pltpu.make_async_remote_copy(
            src_ref=mine_v,
            dst_ref=index_v.at[me],
            send_sem=index_send_sem,
            recv_sem=index_recv_sem,
            device_id=(to, day),
            device_id_type=MESH,
        )

    def floor_of(j):
        odd_lane = lax.broadcasted_iota(jnp.int32, (2 * ROWS, 128), 1) % 2 == 1
        total = jnp.sum(squares[j], axis=-1, keepdims=True)
        odd = jnp.sum(jnp.where(odd_lane, sums[j], 0.0), axis=-1, keepdims=True)
        plain = jnp.sum(jnp.where(odd_lane, 0.0, sums[j]), axis=-1, keepdims=True)
        power = jnp.maximum(1024.0 * total - 2.0 * odd * plain, 0.0)
        return power * (0.02 / (2 * F)) + 1e-06

    for j in range(NJ):
        floor = floor_of(j)

        def whiten(step):
            u = lax.rem(my_u + step, NU)
            if j == 0:
                tab_copy(step).wait()
            spec[...] = jnp.dot(xs[j], tab[u], preferred_element_type=jnp.float32)
            parts = []
            for d in range(2):
                real = spec[d * ROWS : (d + 1) * ROWS, :128]
                imag = spec[d * ROWS : (d + 1) * ROWS, 128:]
                scale = lax.rsqrt(real * real + imag * imag + floor[d * ROWS : (d + 1) * ROWS])
                parts.append((real * scale, imag * scale))
            (re0, im0), (re1, im1) = parts
            re1 = jnp.where(even, pltpu.roll(re1, 96, 1), pltpu.roll(re1, 32, 1))
            im0 = pltpu.roll(im0, 64, 1)
            im1 = jnp.where(even, pltpu.roll(im1, 32, 1), pltpu.roll(im1, 96, 1))
            a, b = jnp.where(even, re0, re1), jnp.where(even, re1, re0)
            c, e = jnp.where(even, im0, im1), jnp.where(even, im1, im0)
            send[j, 4 * u + 0] = jnp.where(low, a, c).astype(jnp.bfloat16)
            send[j, 4 * u + 1] = jnp.where(low, b, e).astype(jnp.bfloat16)
            send[j, 4 * u + 2] = jnp.where(low, c, a).astype(jnp.bfloat16)
            send[j, 4 * u + 3] = jnp.where(low, e, b).astype(jnp.bfloat16)

        def send_four(step):
            u = lax.rem(my_u + step, NU)

            @pl.loop(0, 4)
            def _(q):
                to = 4 * u + q

                @pl.when(to != me)
                def _():
                    block_copy(j, to).start()

        whiten(0)
        if j == 0:
            pl.semaphore_wait(barrier, NC - 1 + ND - 1)
        send_four(0)

        @pl.loop(1, NU)
        def _(step):
            whiten(step)
            send_four(step)

        if j == 0:
            mine_copy.wait()
            index_v[me] = mine_v[...]

            @pl.loop(0, NC - 1)
            def _(i):
                index_copy(peer(i)).start()

            gather_rows((1, 2))

    others = pl.ds(0, NC - 1)
    pltpu.make_async_copy(index_v.at[others], index_v.at[others], index_recv_sem).wait()
    index_to_smem = pltpu.make_async_copy(index_v, index_s, smem_sem)
    index_to_smem.start()
    index_to_smem.wait()

    @pl.loop(0, ND)
    def _(dd):
        @pl.loop(0, NC)
        def _(o):
            for r in range(8):
                for k in range(2):
                    index[dd * 512 + o * 16 + 2 * r + k] = index_s[o, k, dd * 8 + r]

    flip = jnp.where(low, 1.0, -1.0)

    def arrive(j, to):
        @pl.loop(0, NC)
        def _(i):
            source = lax.rem(my_u - i // 4 + NU, NU) * 4 + lax.rem(i, 4)

            def store(rows):
                rows = rows.astype(jnp.float32)
                turned = pltpu.roll(rows, 64, 1)
                four = (jnp.where(low, rows, turned), jnp.where(low, turned, rows), rows * flip, turned)
                for c in range(CH):
                    for k, form in enumerate(four):
                        forms[to, (source * CH + c) * 4 + k] = form[c * SEG : (c + 1) * SEG]

            @pl.when(source != me)
            def _():
                pltpu.make_async_copy(
                    send.at[j, source], recv.at[j, source], recv_sem.at[j, source]
                ).wait()
                store(recv[j, source])

            @pl.when(source == me)
            def _():
                store(send[j, me])

    sign = jnp.where(low, 1.0, 1.0 - 2.0 * (lax.rem(me, 4) // 2).astype(jnp.float32))
    unroll = 32

    def group(dd, chunks):
        @pl.loop(0, 256 // unroll)
        def _(i):
            for r in range(unroll):
                at = dd * 512 + i * (2 * unroll) + 2 * r
                first, second = index[at], index[at + 1]
                total = None
                for j in range(chunks):
                    value = forms[j, first] * forms[j, second + 2]
                    value += forms[j, first + 1] * forms[j, second + 3]
                    total = value if total is None else total + value
                acc[pl.ds(pl.multiple_of((i * unroll + r) * 8, 8), 8), :] = total

        halves = []
        for half in range(2):
            total = acc[pl.ds(half * 1024, ROWS, stride=8), :]
            for s in range(1, 8):
                total = total + acc[pl.ds(half * 1024 + s, ROWS, stride=8), :]
            total = total * sign
            halves.append(total + pltpu.roll(total, 32 if half else 96, 1))
        return jnp.where(even, halves[0], halves[1])

    arrive(0, 0)
    arrive(1, 1)

    def day_copy(to, source, target, send_sem, recv_sem):
        return pltpu.make_async_remote_copy(
            src_ref=source.at[to],
            dst_ref=target.at[day],
            send_sem=send_sem,
            recv_sem=recv_sem.at[day],
            device_id=(me, to),
            device_id_type=MESH,
        )

    def day_at(i):
        x = lax.rem(day // 2 + alternate(4, i // 2), 4)
        return x * 2 + lax.rem(day + 1 + i, 2)

    @pl.loop(0, ND)
    def _(i):
        dd = day_at(i)
        day_send[dd] = group(dd, 2)

        @pl.when(dd != day)
        def _():
            day_copy(dd, day_send, day_recv, day_send_sem, day_recv_sem).start()

    arrive(2, 0)

    @pl.loop(0, ND)
    def _(i):
        dd = day_at(i)
        last = group(dd, 1)

        @pl.when(dd != day)
        def _():
            last_send[dd] = last.astype(jnp.bfloat16)
            day_copy(dd, last_send, last_recv, last_send_sem, last_recv_sem).start()

        @pl.when(dd == day)
        def _():
            own_send[...] = (day_send[day] + last).reshape(16, 8, 128)

    @pl.loop(0, ND - 1)
    def _(i):
        source = day_at(i)
        pltpu.make_async_copy(day_send.at[source], day_recv.at[source], day_recv_sem.at[source]).wait()
        pltpu.make_async_copy(last_send.at[source], last_recv.at[source], last_recv_sem.at[source]).wait()
        value = day_recv[source] + last_recv[source].astype(jnp.float32)
        own_send[...] = own_send[...] + value.reshape(16, 8, 128)

    def own_copy(to):
        return pltpu.make_async_remote_copy(
            src_ref=own_send.at[lax.rem(to, 16)],
            dst_ref=own_recv.at[me],
            send_sem=own_send_sem,
            recv_sem=own_recv_sem,
            device_id=(to, day),
            device_id_type=MESH,
        )

    @pl.loop(0, NC - 1)
    def _(i):
        own_copy(peer(i)).start()

    own_recv[me] = own_send[lax.rem(me, 16)]

    pltpu.make_async_copy(own_recv.at[others], own_recv.at[others], own_recv_sem).wait()

    upper = (jnp.zeros((8, 128), jnp.int32) + me) >= 16
    for t in range(16):
        one, two = own_recv[2 * t], own_recv[2 * t + 1]
        one = jnp.where(upper, pltpu.roll(one, 96, 1), one)
        two = jnp.where(upper, two, pltpu.roll(two, 32, 1))
        value = jnp.where(even[:8], one, two)
        high = value.astype(jnp.bfloat16).astype(jnp.float32)
        lhs[:, t * 128 : (t + 1) * 128] = jnp.concatenate([high, value - high], axis=0).astype(jnp.bfloat16)

    lag_copy.wait()
    lagged = jnp.dot(lhs[...], lag[0], preferred_element_type=jnp.float32) + jnp.dot(
        lhs[...], lag[1], preferred_element_type=jnp.float32
    )
    out[...] = (lagged[:8] + lagged[8:]) * (1.0 / math.sqrt(2.0 * 16 * 24 * F))

    for j in range(NJ):
        pltpu.make_async_copy(send.at[j, others], recv.at[j, others], send_sem.at[j]).wait()
    pltpu.make_async_copy(index_v.at[others], index_v.at[others], index_send_sem).wait()
    pltpu.make_async_copy(own_recv.at[others], own_recv.at[others], own_send_sem).wait()
    days = pl.ds(0, ND - 1)
    pltpu.make_async_copy(day_send.at[days], day_recv.at[days], day_send_sem).wait()
    pltpu.make_async_copy(last_send.at[days], last_recv.at[days], last_send_sem).wait()


def body(segment_records, block_requests, pair_slots):
    bf16, f32, i32 = jnp.bfloat16, jnp.float32, jnp.int32
    dma = pltpu.SemaphoreType.DMA
    return pl.pallas_call(
        kernel,
        out_shape=jax.ShapeDtypeStruct((8, LAGS), f32),
        in_specs=[
            pl.BlockSpec(memory_space=pl.ANY),
            pl.BlockSpec(memory_space=pl.ANY),
            pl.BlockSpec(memory_space=pl.ANY),
            pl.BlockSpec(memory_space=pl.ANY),
            pl.BlockSpec(memory_space=pl.ANY),
            pl.BlockSpec(memory_space=pl.ANY),
        ],
        out_specs=pl.BlockSpec(memory_space=pltpu.VMEM),
        scratch_shapes=[
            pltpu.SMEM((NC, 2, NC), i32),
            pltpu.SMEM((2, 64), i32),
            pltpu.VMEM((768, L), bf16),
            pltpu.VMEM((NJ, 256, L), bf16),
            pltpu.VMEM((8, L), f32),
            pltpu.VMEM((NJ, 256, 128), f32),
            pltpu.VMEM((NJ, 256, 128), f32),
            pltpu.VMEM((NU, L, 256), bf16),
            pltpu.VMEM((256, 256), f32),
            pltpu.VMEM((NJ, NC, ROWS, 128), bf16),
            pltpu.VMEM((NJ, NC, ROWS, 128), bf16),
            pltpu.VMEM((2, 2 * F, LAGS), bf16),
            pltpu.SMEM((2, 64), i32),
            pltpu.VMEM((2, 64), i32),
            pltpu.VMEM((NC, 2, 64), i32),
            pltpu.SMEM((NC, 2, 64), i32),
            pltpu.SMEM((4096,), i32),
            pltpu.VMEM((2, NC * CH * 4, SEG, 128), f32),
            pltpu.VMEM((2048, 128), f32),
            pltpu.VMEM((ND, ROWS, 128), f32),
            pltpu.VMEM((ND, ROWS, 128), f32),
            pltpu.VMEM((ND, ROWS, 128), bf16),
            pltpu.VMEM((ND, ROWS, 128), bf16),
            pltpu.VMEM((16, 8, 128), f32),
            pltpu.VMEM((NC, 8, 128), f32),
            pltpu.VMEM((16, 2 * F), bf16),
            dma((2,)), dma, dma, dma((NU,)), dma, dma((NJ,)), dma((NJ, NC)), dma, dma, dma,
            dma, dma((ND,)), dma, dma((ND,)), dma, dma,
        ],
        compiler_params=pltpu.CompilerParams(
            collective_id=0, has_side_effects=True, vmem_limit_bytes=60 * 2**20
        ),
        name="correlate",
    )(
        block_requests.transpose(0, 2, 1),
        pair_slots.T,
        segment_records.reshape(768, L),
        jnp.asarray(taper_rows()),
        jnp.asarray(forward_blocks()),
        jnp.asarray(lag_rows()),
    )


def solution(mesh):
    return jax.shard_map(
        body,
        mesh=mesh,
        in_specs=(P("day", "chan", None, None), P(), P("chan", None)),
        out_specs=P(("chan", "day"), None),
        check_vma=False,
    )
```

```python
import math

import jax
import jax.numpy as jnp
import numpy as np
from jax import lax
from jax.experimental import pallas as pl
from jax.experimental.pallas import tpu as pltpu
from jax.sharding import PartitionSpec as P

L = 2048
F = 1024
LAGS = 256
MESH = pl.DeviceIdType.MESH
NC = 32
BINS = F // NC
NU = NC // 4
NJ = 3
SEG = 8
CH = 16
ROWS = CH * SEG
ND = 8


def forward_blocks():
    n = np.arange(L, dtype=np.int64)[:, None]
    k = np.arange(1, F + 1, dtype=np.int64)[None, :]
    phase = (n * k % L).astype(np.float32) * np.float32(2.0 * math.pi / L)
    taper = np.float32(0.5) - np.float32(0.5) * np.cos(
        np.arange(L, dtype=np.float32) * np.float32(2.0 * math.pi / L)
    )
    real = (taper[:, None] * np.cos(phase)).reshape(L, NU, 4, BINS)
    imag = (-taper[:, None] * np.sin(phase)).reshape(L, NU, 4, BINS)
    both = np.stack([real, imag], axis=2).reshape(L, NU, 256)
    return np.ascontiguousarray(both.transpose(1, 0, 2)).astype(jnp.bfloat16)


def taper_rows():
    n = np.arange(L, dtype=np.float32)
    taper = np.float32(0.5) - np.float32(0.5) * np.cos(n * np.float32(2.0 * math.pi / L))
    return np.broadcast_to(taper, (8, L)).copy()


def lag_rows():
    k = np.arange(1, F + 1, dtype=np.int64)[:, None]
    t = np.arange(LAGS, dtype=np.int64)[None, :] - LAGS // 2
    phase = (k * t % L).astype(np.float32) * np.float32(2.0 * math.pi / L)
    shape = (NC // 2, 2, BINS, LAGS)
    both = np.stack([np.cos(phase).reshape(shape), -np.sin(phase).reshape(shape)], axis=1)
    both = both.reshape(2 * F, LAGS).astype(np.float32)
    high = both.astype(jnp.bfloat16)
    return np.stack([high, (both - high.astype(np.float32)).astype(jnp.bfloat16)])


def alternate(count, step):
    return count // 2 + (1 - 2 * lax.rem(step, 2)) * ((step + 1) // 2)


def kernel(
    req_hbm, slots_hbm, x_hbm, taper_hbm, tab_hbm, lag_hbm, out,
    req, slots, xv, xs, taper, squares, sums, tab, spec, send, recv, lag, mine_s, mine_v, index_v, index_s, index, forms, acc,
    day_send, day_recv, last_send, last_recv, own_send, own_recv, lhs,
    in_sem, x_sem, taper_sem, tab_sem, lag_sem, send_sem, recv_sem, index_send_sem, index_recv_sem, smem_sem,
    day_send_sem, day_recv_sem, last_send_sem, last_recv_sem, own_send_sem, own_recv_sem,
):
    me = lax.axis_index("chan")
    day = lax.axis_index("day")
    my_u = me // 4
    lane = lax.broadcasted_iota(jnp.int32, (ROWS, 128), 1)
    even = lane % 64 < 32
    low = lane < 64

    def peer(step):
        y = lax.rem(me // 8 + alternate(4, lax.rem(step, 4)), 4)
        z = lax.rem(lax.rem(me, 8) + alternate(8, step // 4), 8)
        return y * 8 + z

    x_copy = pltpu.make_async_copy(x_hbm, xv, x_sem)
    x_copy.start()
    taper_copy = pltpu.make_async_copy(taper_hbm, taper, taper_sem)
    taper_copy.start()
    slots_copy = pltpu.make_async_copy(slots_hbm, slots, in_sem.at[0])
    slots_copy.start()
    req_copy = pltpu.make_async_copy(req_hbm, req, in_sem.at[1])
    req_copy.start()

    barrier = pltpu.get_barrier_semaphore()

    @pl.loop(0, NC - 1)
    def _(i):
        pl.semaphore_signal(barrier, inc=1, device_id=(peer(i), day), device_id_type=MESH)

    @pl.loop(1, ND)
    def _(i):
        pl.semaphore_signal(
            barrier, inc=1, device_id=(me, lax.rem(day + i, ND)), device_id_type=MESH
        )

    def tab_copy(step):
        u = lax.rem(my_u + step, NU)
        return pltpu.make_async_copy(tab_hbm.at[u], tab.at[u], tab_sem.at[u])

    @pl.loop(0, NU)
    def _(step):
        tab_copy(step).start()

    lag_copy = pltpu.make_async_copy(lag_hbm, lag, lag_sem)
    lag_copy.start()

    slots_copy.wait()
    req_copy.wait()

    @pl.loop(0, 64)
    def _(i):
        for k in range(2):
            slot = slots[k, i]
            source = slot >> 1
            mine_s[k, i] = (source * CH + req[me, slot & 1, source]) * 4

    mine_copy = pltpu.make_async_copy(mine_s, mine_v, smem_sem)
    mine_copy.start()

    taper_copy.wait()
    x_copy.wait()

    def gather_rows(chunks):
        @pl.loop(0, 16)
        def _(i):
            rows = xv[pl.ds(pl.multiple_of(i * 48, 16), 48), :].astype(jnp.float32)
            rows = rows.reshape(2, NJ, SEG, L)
            at = pl.ds(pl.multiple_of(i * 16, 16), 16)
            for j in chunks:
                xs[j, at, :] = rows[:, j].reshape(16, L).astype(jnp.bfloat16)
                for half in range(2):
                    tapered = rows[half, j] * taper[...]
                    square = plain = None
                    for t in range(L // 128):
                        part = tapered[:, t * 128 : (t + 1) * 128]
                        square = part * part if t == 0 else square + part * part
                        plain = part if t == 0 else plain + part
                    low_at = pl.ds(pl.multiple_of(i * 16 + half * 8, 8), 8)
                    squares[j, low_at, :] = square
                    sums[j, low_at, :] = plain

    gather_rows((0,))

    def block_copy(j, to):
        return pltpu.make_async_remote_copy(
            src_ref=send.at[j, to],
            dst_ref=recv.at[j, me],
            send_sem=send_sem.at[j],
            recv_sem=recv_sem.at[j, me],
            device_id=(to, day),
            device_id_type=MESH,
        )

    def index_copy(to):
        return pltpu.make_async_remote_copy(
            src_ref=mine_v,
            dst_ref=index_v.at[me],
            send_sem=index_send_sem,
            recv_sem=index_recv_sem,
            device_id=(to, day),
            device_id_type=MESH,
        )

    def floor_of(j):
        odd_lane = lax.broadcasted_iota(jnp.int32, (2 * ROWS, 128), 1) % 2 == 1
        total = jnp.sum(squares[j], axis=-1, keepdims=True)
        odd = jnp.sum(jnp.where(odd_lane, sums[j], 0.0), axis=-1, keepdims=True)
        plain = jnp.sum(jnp.where(odd_lane, 0.0, sums[j]), axis=-1, keepdims=True)
        mean = jnp.maximum(0.5 * total - odd * (plain * (1.0 / F)), 0.0)
        return 0.02 * mean + 1e-06

    for j in range(NJ):
        floor = floor_of(j)

        def whiten(step):
            u = lax.rem(my_u + step, NU)
            if j == 0:
                tab_copy(step).wait()
            spec[...] = jnp.dot(xs[j], tab[u], preferred_element_type=jnp.float32)
            parts = []
            for d in range(2):
                real = spec[d * ROWS : (d + 1) * ROWS, :128]
                imag = spec[d * ROWS : (d + 1) * ROWS, 128:]
                scale = lax.rsqrt(real * real + imag * imag + floor[d * ROWS : (d + 1) * ROWS])
                parts.append((real * scale, imag * scale))
            (re0, im0), (re1, im1) = parts
            re1 = jnp.where(even, pltpu.roll(re1, 96, 1), pltpu.roll(re1, 32, 1))
            im0 = pltpu.roll(im0, 64, 1)
            im1 = jnp.where(even, pltpu.roll(im1, 32, 1), pltpu.roll(im1, 96, 1))
            a, b = jnp.where(even, re0, re1), jnp.where(even, re1, re0)
            c, e = jnp.where(even, im0, im1), jnp.where(even, im1, im0)
            send[j, 4 * u + 0] = jnp.where(low, a, c).astype(jnp.bfloat16)
            send[j, 4 * u + 1] = jnp.where(low, b, e).astype(jnp.bfloat16)
            send[j, 4 * u + 2] = jnp.where(low, c, a).astype(jnp.bfloat16)
            send[j, 4 * u + 3] = jnp.where(low, e, b).astype(jnp.bfloat16)

        def send_four(step):
            u = lax.rem(my_u + step, NU)

            @pl.loop(0, 4)
            def _(q):
                to = 4 * u + q

                @pl.when(to != me)
                def _():
                    block_copy(j, to).start()

        whiten(0)
        whiten(1)
        if j == 0:
            pl.semaphore_wait(barrier, NC - 1 + ND - 1)
        send_four(0)
        send_four(1)

        @pl.loop(2, NU)
        def _(step):
            whiten(step)
            send_four(step)

        if j == 0:
            mine_copy.wait()
            index_v[me] = mine_v[...]

            @pl.loop(0, NC - 1)
            def _(i):
                index_copy(peer(i)).start()

            gather_rows((1, 2))

    others = pl.ds(0, NC - 1)
    pltpu.make_async_copy(index_v.at[others], index_v.at[others], index_recv_sem).wait()
    index_to_smem = pltpu.make_async_copy(index_v, index_s, smem_sem)
    index_to_smem.start()
    index_to_smem.wait()

    @pl.loop(0, ND)
    def _(dd):
        @pl.loop(0, NC)
        def _(o):
            for r in range(8):
                for k in range(2):
                    index[dd * 512 + o * 16 + 2 * r + k] = index_s[o, k, dd * 8 + r]

    flip = jnp.where(low, 1.0, -1.0)

    def arrive(j, to):
        @pl.loop(0, NC)
        def _(i):
            source = lax.rem(my_u - i // 4 + NU, NU) * 4 + lax.rem(i, 4)

            def store(rows):
                rows = rows.astype(jnp.float32)
                turned = pltpu.roll(rows, 64, 1)
                four = (jnp.where(low, rows, turned), jnp.where(low, turned, rows), rows * flip, turned)
                for c in range(CH):
                    for k, form in enumerate(four):
                        forms[to, (source * CH + c) * 4 + k] = form[c * SEG : (c + 1) * SEG]

            @pl.when(source != me)
            def _():
                pltpu.make_async_copy(
                    send.at[j, source], recv.at[j, source], recv_sem.at[j, source]
                ).wait()
                store(recv[j, source])

            @pl.when(source == me)
            def _():
                store(send[j, me])

    sign = jnp.where(low, 1.0, 1.0 - 2.0 * (lax.rem(me, 4) // 2).astype(jnp.float32))
    unroll = 32

    def group(dd, chunks):
        @pl.loop(0, 256 // unroll)
        def _(i):
            for r in range(unroll):
                at = dd * 512 + i * (2 * unroll) + 2 * r
                first, second = index[at], index[at + 1]
                total = None
                for j in range(chunks):
                    value = forms[j, first] * forms[j, second + 2]
                    value += forms[j, first + 1] * forms[j, second + 3]
                    total = value if total is None else total + value
                acc[pl.ds(pl.multiple_of((i * unroll + r) * 8, 8), 8), :] = total

        halves = []
        for half in range(2):
            total = acc[pl.ds(half * 1024, ROWS, stride=8), :]
            for s in range(1, 8):
                total = total + acc[pl.ds(half * 1024 + s, ROWS, stride=8), :]
            total = total * sign
            halves.append(total + pltpu.roll(total, 32 if half else 96, 1))
        return jnp.where(even, halves[0], halves[1])

    arrive(0, 0)
    arrive(1, 1)

    def day_copy(to, source, target, send_sem, recv_sem):
        return pltpu.make_async_remote_copy(
            src_ref=source.at[to],
            dst_ref=target.at[day],
            send_sem=send_sem,
            recv_sem=recv_sem.at[day],
            device_id=(me, to),
            device_id_type=MESH,
        )

    def day_at(i):
        x = lax.rem(day // 2 + alternate(4, i // 2), 4)
        return x * 2 + lax.rem(day + 1 + i, 2)

    @pl.loop(0, ND)
    def _(i):
        dd = day_at(i)
        day_send[dd] = group(dd, 2)

        @pl.when(dd != day)
        def _():
            day_copy(dd, day_send, day_recv, day_send_sem, day_recv_sem).start()

    arrive(2, 0)

    @pl.loop(0, ND)
    def _(i):
        dd = day_at(i)
        last = group(dd, 1)

        @pl.when(dd != day)
        def _():
            last_send[dd] = last.astype(jnp.bfloat16)
            day_copy(dd, last_send, last_recv, last_send_sem, last_recv_sem).start()

        @pl.when(dd == day)
        def _():
            own_send[...] = (day_send[day] + last).reshape(16, 8, 128)

    @pl.loop(0, ND - 1)
    def _(i):
        source = day_at(i)
        pltpu.make_async_copy(day_send.at[source], day_recv.at[source], day_recv_sem.at[source]).wait()
        pltpu.make_async_copy(last_send.at[source], last_recv.at[source], last_recv_sem.at[source]).wait()
        value = day_recv[source] + last_recv[source].astype(jnp.float32)
        own_send[...] = own_send[...] + value.reshape(16, 8, 128)

    def own_copy(to):
        return pltpu.make_async_remote_copy(
            src_ref=own_send.at[lax.rem(to, 16)],
            dst_ref=own_recv.at[me],
            send_sem=own_send_sem,
            recv_sem=own_recv_sem,
            device_id=(to, day),
            device_id_type=MESH,
        )

    @pl.loop(0, NC - 1)
    def _(i):
        own_copy(peer(i)).start()

    own_recv[me] = own_send[lax.rem(me, 16)]

    pltpu.make_async_copy(own_recv.at[others], own_recv.at[others], own_recv_sem).wait()

    upper = (jnp.zeros((8, 128), jnp.int32) + me) >= 16
    for t in range(16):
        one, two = own_recv[2 * t], own_recv[2 * t + 1]
        one = jnp.where(upper, pltpu.roll(one, 96, 1), one)
        two = jnp.where(upper, two, pltpu.roll(two, 32, 1))
        value = jnp.where(even[:8], one, two)
        high = value.astype(jnp.bfloat16).astype(jnp.float32)
        lhs[:, t * 128 : (t + 1) * 128] = jnp.concatenate([high, value - high], axis=0).astype(jnp.bfloat16)

    lag_copy.wait()
    lagged = jnp.dot(lhs[...], lag[0], preferred_element_type=jnp.float32) + jnp.dot(
        lhs[...], lag[1], preferred_element_type=jnp.float32
    )
    out[...] = (lagged[:8] + lagged[8:]) * (1.0 / math.sqrt(2.0 * 16 * 24 * F))

    for j in range(NJ):
        pltpu.make_async_copy(send.at[j, others], recv.at[j, others], send_sem.at[j]).wait()
    pltpu.make_async_copy(index_v.at[others], index_v.at[others], index_send_sem).wait()
    pltpu.make_async_copy(own_recv.at[others], own_recv.at[others], own_send_sem).wait()
    days = pl.ds(0, ND - 1)
    pltpu.make_async_copy(day_send.at[days], day_recv.at[days], day_send_sem).wait()
    pltpu.make_async_copy(last_send.at[days], last_recv.at[days], last_send_sem).wait()


def body(segment_records, block_requests, pair_slots):
    bf16, f32, i32 = jnp.bfloat16, jnp.float32, jnp.int32
    dma = pltpu.SemaphoreType.DMA
    return pl.pallas_call(
        kernel,
        out_shape=jax.ShapeDtypeStruct((8, LAGS), f32),
        in_specs=[
            pl.BlockSpec(memory_space=pl.ANY),
            pl.BlockSpec(memory_space=pl.ANY),
            pl.BlockSpec(memory_space=pl.ANY),
            pl.BlockSpec(memory_space=pl.ANY),
            pl.BlockSpec(memory_space=pl.ANY),
            pl.BlockSpec(memory_space=pl.ANY),
        ],
        out_specs=pl.BlockSpec(memory_space=pltpu.VMEM),
        scratch_shapes=[
            pltpu.SMEM((NC, 2, NC), i32),
            pltpu.SMEM((2, 64), i32),
            pltpu.VMEM((768, L), bf16),
            pltpu.VMEM((NJ, 256, L), bf16),
            pltpu.VMEM((8, L), f32),
            pltpu.VMEM((NJ, 256, 128), f32),
            pltpu.VMEM((NJ, 256, 128), f32),
            pltpu.VMEM((NU, L, 256), bf16),
            pltpu.VMEM((256, 256), f32),
            pltpu.VMEM((NJ, NC, ROWS, 128), bf16),
            pltpu.VMEM((NJ, NC, ROWS, 128), bf16),
            pltpu.VMEM((2, 2 * F, LAGS), bf16),
            pltpu.SMEM((2, 64), i32),
            pltpu.VMEM((2, 64), i32),
            pltpu.VMEM((NC, 2, 64), i32),
            pltpu.SMEM((NC, 2, 64), i32),
            pltpu.SMEM((4096,), i32),
            pltpu.VMEM((2, NC * CH * 4, SEG, 128), f32),
            pltpu.VMEM((2048, 128), f32),
            pltpu.VMEM((ND, ROWS, 128), f32),
            pltpu.VMEM((ND, ROWS, 128), f32),
            pltpu.VMEM((ND, ROWS, 128), bf16),
            pltpu.VMEM((ND, ROWS, 128), bf16),
            pltpu.VMEM((16, 8, 128), f32),
            pltpu.VMEM((NC, 8, 128), f32),
            pltpu.VMEM((16, 2 * F), bf16),
            dma((2,)), dma, dma, dma((NU,)), dma, dma((NJ,)), dma((NJ, NC)), dma, dma, dma,
            dma, dma((ND,)), dma, dma((ND,)), dma, dma,
        ],
        compiler_params=pltpu.CompilerParams(
            collective_id=0, has_side_effects=True, vmem_limit_bytes=60 * 2**20
        ),
        name="correlate",
    )(
        block_requests.transpose(0, 2, 1),
        pair_slots.T,
        segment_records.reshape(768, L),
        jnp.asarray(taper_rows()),
        jnp.asarray(forward_blocks()),
        jnp.asarray(lag_rows()),
    )


def solution(mesh):
    return jax.shard_map(
        body,
        mesh=mesh,
        in_specs=(P("day", "chan", None, None), P(), P("chan", None)),
        out_specs=P(("chan", "day"), None),
        check_vma=False,
    )
```

```python
import math

import jax
import jax.numpy as jnp
import numpy as np
from jax import lax
from jax.experimental import pallas as pl
from jax.experimental.pallas import tpu as pltpu
from jax.sharding import PartitionSpec as P

L = 2048
F = 1024
LAGS = 256
MESH = pl.DeviceIdType.MESH
NC = 32
BINS = F // NC
NU = NC // 4
NJ = 3
SEG = 8
CH = 16
ROWS = CH * SEG
ND = 8


def forward_blocks():
    n = np.arange(L, dtype=np.int64)[:, None]
    k = np.arange(1, F + 1, dtype=np.int64)[None, :]
    phase = (n * k % L).astype(np.float32) * np.float32(2.0 * math.pi / L)
    taper = np.float32(0.5) - np.float32(0.5) * np.cos(
        np.arange(L, dtype=np.float32) * np.float32(2.0 * math.pi / L)
    )
    real = (taper[:, None] * np.cos(phase)).reshape(L, NU, 4, BINS)
    imag = (-taper[:, None] * np.sin(phase)).reshape(L, NU, 4, BINS)
    both = np.stack([real, imag], axis=2).reshape(L, NU, 256)
    return np.ascontiguousarray(both.transpose(1, 0, 2)).astype(jnp.bfloat16)


def taper_rows():
    n = np.arange(L, dtype=np.float32)
    taper = np.float32(0.5) - np.float32(0.5) * np.cos(n * np.float32(2.0 * math.pi / L))
    return np.broadcast_to(taper, (8, L)).copy()


def lag_rows():
    k = np.arange(1, F + 1, dtype=np.int64)[:, None]
    t = np.arange(LAGS, dtype=np.int64)[None, :] - LAGS // 2
    phase = (k * t % L).astype(np.float32) * np.float32(2.0 * math.pi / L)
    shape = (NC // 2, 2, BINS, LAGS)
    both = np.stack([np.cos(phase).reshape(shape), -np.sin(phase).reshape(shape)], axis=1)
    both = both.reshape(2 * F, LAGS).astype(np.float32)
    high = both.astype(jnp.bfloat16)
    return np.stack([high, (both - high.astype(np.float32)).astype(jnp.bfloat16)])


def alternate(count, step):
    return count // 2 + (1 - 2 * lax.rem(step, 2)) * ((step + 1) // 2)


def kernel(
    req_hbm, slots_hbm, x_hbm, taper_hbm, tab_hbm, lag_hbm, out,
    req, slots, xv, xs, taper, squares, sums, tab, spec, send, recv, lag, mine_s, mine_v, index_v, index_s, index, forms, acc,
    day_send, day_recv, last_send, last_recv, own_send, own_recv, lhs,
    in_sem, x_sem, taper_sem, tab_sem, lag_sem, send_sem, recv_sem, index_send_sem, index_recv_sem, smem_sem,
    day_send_sem, day_recv_sem, last_send_sem, last_recv_sem, own_send_sem, own_recv_sem,
):
    me = lax.axis_index("chan")
    day = lax.axis_index("day")
    my_u = me // 4
    lane = lax.broadcasted_iota(jnp.int32, (ROWS, 128), 1)
    even = lane % 64 < 32
    low = lane < 64

    def peer(step):
        y = lax.rem(me // 8 + alternate(4, lax.rem(step, 4)), 4)
        z = lax.rem(lax.rem(me, 8) + alternate(8, step // 4), 8)
        return y * 8 + z

    x_copy = pltpu.make_async_copy(x_hbm, xv, x_sem)
    x_copy.start()
    taper_copy = pltpu.make_async_copy(taper_hbm, taper, taper_sem)
    taper_copy.start()
    slots_copy = pltpu.make_async_copy(slots_hbm, slots, in_sem.at[0])
    slots_copy.start()
    req_copy = pltpu.make_async_copy(req_hbm, req, in_sem.at[1])
    req_copy.start()

    barrier = pltpu.get_barrier_semaphore()

    @pl.loop(0, NC - 1)
    def _(i):
        pl.semaphore_signal(barrier, inc=1, device_id=(peer(i), day), device_id_type=MESH)

    @pl.loop(1, ND)
    def _(i):
        pl.semaphore_signal(
            barrier, inc=1, device_id=(me, lax.rem(day + i, ND)), device_id_type=MESH
        )

    def tab_copy(step):
        u = lax.rem(my_u + step, NU)
        return pltpu.make_async_copy(tab_hbm.at[u], tab.at[u], tab_sem.at[u])

    @pl.loop(0, NU)
    def _(step):
        tab_copy(step).start()

    lag_copy = pltpu.make_async_copy(lag_hbm, lag, lag_sem)
    lag_copy.start()

    slots_copy.wait()
    req_copy.wait()

    @pl.loop(0, 64)
    def _(i):
        for k in range(2):
            slot = slots[k, i]
            source = slot >> 1
            mine_s[k, i] = (source * CH + req[me, slot & 1, source]) * 4

    mine_copy = pltpu.make_async_copy(mine_s, mine_v, smem_sem)
    mine_copy.start()

    taper_copy.wait()
    x_copy.wait()

    def gather_rows(chunks):
        @pl.loop(0, 16)
        def _(i):
            rows = xv[pl.ds(pl.multiple_of(i * 48, 16), 48), :].astype(jnp.float32)
            rows = rows.reshape(2, NJ, SEG, L)
            at = pl.ds(pl.multiple_of(i * 16, 16), 16)
            for j in chunks:
                xs[j, at, :] = rows[:, j].reshape(16, L).astype(jnp.bfloat16)
                for half in range(2):
                    tapered = rows[half, j] * taper[...]
                    square = plain = None
                    for t in range(L // 128):
                        part = tapered[:, t * 128 : (t + 1) * 128]
                        square = part * part if t == 0 else square + part * part
                        plain = part if t == 0 else plain + part
                    low_at = pl.ds(pl.multiple_of(i * 16 + half * 8, 8), 8)
                    squares[j, low_at, :] = square
                    sums[j, low_at, :] = plain

    gather_rows((0,))

    def block_copy(j, to):
        return pltpu.make_async_remote_copy(
            src_ref=send.at[j, to],
            dst_ref=recv.at[j, me],
            send_sem=send_sem.at[j],
            recv_sem=recv_sem.at[j, me],
            device_id=(to, day),
            device_id_type=MESH,
        )

    def index_copy(to):
        return pltpu.make_async_remote_copy(
            src_ref=mine_v,
            dst_ref=index_v.at[me],
            send_sem=index_send_sem,
            recv_sem=index_recv_sem,
            device_id=(to, day),
            device_id_type=MESH,
        )

    def floor_of(j):
        odd_lane = lax.broadcasted_iota(jnp.int32, (2 * ROWS, 128), 1) % 2 == 1
        total = jnp.sum(squares[j], axis=-1, keepdims=True)
        odd = jnp.sum(jnp.where(odd_lane, sums[j], 0.0), axis=-1, keepdims=True)
        plain = jnp.sum(jnp.where(odd_lane, 0.0, sums[j]), axis=-1, keepdims=True)
        mean = jnp.maximum(0.5 * total - odd * (plain * (1.0 / F)), 0.0)
        return 0.02 * mean + 1e-06

    for j in range(NJ):
        floor = floor_of(j)

        def whiten(step):
            u = lax.rem(my_u + step, NU)
            if j == 0:
                tab_copy(step).wait()
            spec[...] = jnp.dot(xs[j], tab[u], preferred_element_type=jnp.float32)
            parts = []
            for d in range(2):
                real = spec[d * ROWS : (d + 1) * ROWS, :128]
                imag = spec[d * ROWS : (d + 1) * ROWS, 128:]
                scale = lax.rsqrt(real * real + imag * imag + floor[d * ROWS : (d + 1) * ROWS])
                parts.append((real * scale, imag * scale))
            (re0, im0), (re1, im1) = parts
            re1 = jnp.where(even, pltpu.roll(re1, 96, 1), pltpu.roll(re1, 32, 1))
            im0 = pltpu.roll(im0, 64, 1)
            im1 = jnp.where(even, pltpu.roll(im1, 32, 1), pltpu.roll(im1, 96, 1))
            a, b = jnp.where(even, re0, re1), jnp.where(even, re1, re0)
            c, e = jnp.where(even, im0, im1), jnp.where(even, im1, im0)
            send[j, 4 * u + 0] = jnp.where(low, a, c).astype(jnp.bfloat16)
            send[j, 4 * u + 1] = jnp.where(low, b, e).astype(jnp.bfloat16)
            send[j, 4 * u + 2] = jnp.where(low, c, a).astype(jnp.bfloat16)
            send[j, 4 * u + 3] = jnp.where(low, e, b).astype(jnp.bfloat16)

        def send_four(step):
            u = lax.rem(my_u + step, NU)

            @pl.loop(0, 4)
            def _(q):
                to = 4 * u + q

                @pl.when(to != me)
                def _():
                    block_copy(j, to).start()

        whiten(0)
        whiten(1)
        if j == 0:
            pl.semaphore_wait(barrier, NC - 1 + ND - 1)
        send_four(0)
        send_four(1)

        @pl.loop(2, NU)
        def _(step):
            whiten(step)
            send_four(step)

        if j == 0:
            mine_copy.wait()
            index_v[me] = mine_v[...]

            @pl.loop(0, NC - 1)
            def _(i):
                index_copy(peer(i)).start()

            gather_rows((1, 2))

    others = pl.ds(0, NC - 1)
    pltpu.make_async_copy(index_v.at[others], index_v.at[others], index_recv_sem).wait()
    index_to_smem = pltpu.make_async_copy(index_v, index_s, smem_sem)
    index_to_smem.start()
    index_to_smem.wait()

    @pl.loop(0, ND)
    def _(dd):
        @pl.loop(0, NC)
        def _(o):
            for r in range(8):
                for k in range(2):
                    index[dd * 512 + o * 16 + 2 * r + k] = index_s[o, k, dd * 8 + r]

    flip = jnp.where(low, 1.0, -1.0)

    def arrive(j, to):
        @pl.loop(0, NC)
        def _(i):
            source = lax.rem(my_u - i // 4 + NU, NU) * 4 + lax.rem(i, 4)

            def store(rows):
                rows = rows.astype(jnp.float32)
                turned = pltpu.roll(rows, 64, 1)
                four = (jnp.where(low, rows, turned), jnp.where(low, turned, rows), rows * flip, turned)
                for c in range(CH):
                    for k, form in enumerate(four):
                        forms[to, (source * CH + c) * 4 + k] = form[c * SEG : (c + 1) * SEG]

            @pl.when(source != me)
            def _():
                pltpu.make_async_copy(
                    send.at[j, source], recv.at[j, source], recv_sem.at[j, source]
                ).wait()
                store(recv[j, source])

            @pl.when(source == me)
            def _():
                store(send[j, me])

    sign = jnp.where(low, 1.0, 1.0 - 2.0 * (lax.rem(me, 4) // 2).astype(jnp.float32))
    unroll = 32

    def group(dd, chunks):
        @pl.loop(0, 256 // unroll)
        def _(i):
            for r in range(unroll):
                at = dd * 512 + i * (2 * unroll) + 2 * r
                first, second = index[at], index[at + 1]
                total = None
                for j in range(chunks):
                    value = forms[j, first] * forms[j, second + 2]
                    value += forms[j, first + 1] * forms[j, second + 3]
                    total = value if total is None else total + value
                acc[pl.ds(pl.multiple_of((i * unroll + r) * 8, 8), 8), :] = total

        halves = []
        for half in range(2):
            total = acc[pl.ds(half * 1024, ROWS, stride=8), :]
            for s in range(1, 8):
                total = total + acc[pl.ds(half * 1024 + s, ROWS, stride=8), :]
            total = total * sign
            halves.append(total + pltpu.roll(total, 32 if half else 96, 1))
        return jnp.where(even, halves[0], halves[1])

    arrive(0, 0)
    arrive(1, 1)

    def day_copy(to, source, target, send_sem, recv_sem):
        return pltpu.make_async_remote_copy(
            src_ref=source.at[to],
            dst_ref=target.at[day],
            send_sem=send_sem,
            recv_sem=recv_sem.at[day],
            device_id=(me, to),
            device_id_type=MESH,
        )

    def day_at(i):
        x = lax.rem(day // 2 + alternate(4, i // 2), 4)
        return x * 2 + lax.rem(day + 1 + i, 2)

    @pl.loop(0, ND)
    def _(i):
        dd = day_at(i)
        day_send[dd] = group(dd, 2)

        @pl.when(dd != day)
        def _():
            day_copy(dd, day_send, day_recv, day_send_sem, day_recv_sem).start()

    arrive(2, 0)

    @pl.loop(0, ND)
    def _(i):
        dd = day_at(i)
        last = group(dd, 1)

        @pl.when(dd != day)
        def _():
            last_send[dd] = last.astype(jnp.bfloat16)
            day_copy(dd, last_send, last_recv, last_send_sem, last_recv_sem).start()

        @pl.when(dd == day)
        def _():
            own_send[...] = (day_send[day] + last).reshape(16, 8, 128)

    @pl.loop(0, ND - 1)
    def _(i):
        source = day_at(i)
        pltpu.make_async_copy(day_send.at[source], day_recv.at[source], day_recv_sem.at[source]).wait()
        pltpu.make_async_copy(last_send.at[source], last_recv.at[source], last_recv_sem.at[source]).wait()
        value = day_recv[source] + last_recv[source].astype(jnp.float32)
        own_send[...] = own_send[...] + value.reshape(16, 8, 128)

    def own_copy(to):
        return pltpu.make_async_remote_copy(
            src_ref=own_send.at[lax.rem(to, 16)],
            dst_ref=own_recv.at[me],
            send_sem=own_send_sem,
            recv_sem=own_recv_sem,
            device_id=(to, day),
            device_id_type=MESH,
        )

    @pl.loop(0, NC - 1)
    def _(i):
        own_copy(peer(i)).start()

    own_recv[me] = own_send[lax.rem(me, 16)]

    pltpu.make_async_copy(own_recv.at[others], own_recv.at[others], own_recv_sem).wait()

    upper = (jnp.zeros((8, 128), jnp.int32) + me) >= 16
    for t in range(16):
        one, two = own_recv[2 * t], own_recv[2 * t + 1]
        one = jnp.where(upper, pltpu.roll(one, 96, 1), one)
        two = jnp.where(upper, two, pltpu.roll(two, 32, 1))
        value = jnp.where(even[:8], one, two)
        high = value.astype(jnp.bfloat16).astype(jnp.float32)
        lhs[:, t * 128 : (t + 1) * 128] = jnp.concatenate([high, value - high], axis=0).astype(jnp.bfloat16)

    lag_copy.wait()
    lagged = jnp.dot(lhs[...], lag[0], preferred_element_type=jnp.float32) + jnp.dot(
        lhs[...], lag[1], preferred_element_type=jnp.float32
    )
    out[...] = lagged[:8] + lagged[8:]

    for j in range(NJ):
        pltpu.make_async_copy(send.at[j, others], recv.at[j, others], send_sem.at[j]).wait()
    pltpu.make_async_copy(index_v.at[others], index_v.at[others], index_send_sem).wait()
    pltpu.make_async_copy(own_recv.at[others], own_recv.at[others], own_send_sem).wait()
    days = pl.ds(0, ND - 1)
    pltpu.make_async_copy(day_send.at[days], day_recv.at[days], day_send_sem).wait()
    pltpu.make_async_copy(last_send.at[days], last_recv.at[days], last_send_sem).wait()


def body(segment_records, block_requests, pair_slots):
    bf16, f32, i32 = jnp.bfloat16, jnp.float32, jnp.int32
    dma = pltpu.SemaphoreType.DMA
    lagged = pl.pallas_call(
        kernel,
        out_shape=jax.ShapeDtypeStruct((8, LAGS), f32),
        in_specs=[
            pl.BlockSpec(memory_space=pl.ANY),
            pl.BlockSpec(memory_space=pl.ANY),
            pl.BlockSpec(memory_space=pl.ANY),
            pl.BlockSpec(memory_space=pl.ANY),
            pl.BlockSpec(memory_space=pl.ANY),
            pl.BlockSpec(memory_space=pl.ANY),
        ],
        out_specs=pl.BlockSpec(memory_space=pltpu.VMEM),
        scratch_shapes=[
            pltpu.SMEM((NC, 2, NC), i32),
            pltpu.SMEM((2, 64), i32),
            pltpu.VMEM((768, L), bf16),
            pltpu.VMEM((NJ, 256, L), bf16),
            pltpu.VMEM((8, L), f32),
            pltpu.VMEM((NJ, 256, 128), f32),
            pltpu.VMEM((NJ, 256, 128), f32),
            pltpu.VMEM((NU, L, 256), bf16),
            pltpu.VMEM((256, 256), f32),
            pltpu.VMEM((NJ, NC, ROWS, 128), bf16),
            pltpu.VMEM((NJ, NC, ROWS, 128), bf16),
            pltpu.VMEM((2, 2 * F, LAGS), bf16),
            pltpu.SMEM((2, 64), i32),
            pltpu.VMEM((2, 64), i32),
            pltpu.VMEM((NC, 2, 64), i32),
            pltpu.SMEM((NC, 2, 64), i32),
            pltpu.SMEM((4096,), i32),
            pltpu.VMEM((2, NC * CH * 4, SEG, 128), f32),
            pltpu.VMEM((2048, 128), f32),
            pltpu.VMEM((ND, ROWS, 128), f32),
            pltpu.VMEM((ND, ROWS, 128), f32),
            pltpu.VMEM((ND, ROWS, 128), bf16),
            pltpu.VMEM((ND, ROWS, 128), bf16),
            pltpu.VMEM((16, 8, 128), f32),
            pltpu.VMEM((NC, 8, 128), f32),
            pltpu.VMEM((16, 2 * F), bf16),
            dma((2,)), dma, dma, dma((NU,)), dma, dma((NJ,)), dma((NJ, NC)), dma, dma, dma,
            dma, dma((ND,)), dma, dma((ND,)), dma, dma,
        ],
        compiler_params=pltpu.CompilerParams(
            collective_id=0, has_side_effects=True, vmem_limit_bytes=60 * 2**20
        ),
        name="correlate",
    )(
        block_requests.transpose(0, 2, 1),
        pair_slots.T,
        segment_records.reshape(768, L),
        jnp.asarray(taper_rows()),
        jnp.asarray(forward_blocks()),
        jnp.asarray(lag_rows()),
    )
    return lagged * (1.0 / math.sqrt(2.0 * 16 * 24 * F))


def solution(mesh):
    return jax.shard_map(
        body,
        mesh=mesh,
        in_specs=(P("day", "chan", None, None), P(), P("chan", None)),
        out_specs=P(("chan", "day"), None),
        check_vma=False,
    )
```
